32 devices in a mesh: sections: 2 (over x), tx: 16 (over z, y, core).
Axes of the slice: x: 2, y: 2, z: 4, core: 2. Of those that a mesh axis runs over, the one named last changes fastest.
Arguments:
- positions: float32 [2, 32768], P(None, ('sections', 'tx')), parts along dimension 1, may hold values from 0 to 128, as said below
- counts: int32 [256], P(('sections', 'tx')), parts along dimension 0, may hold values from 1 to 128, as said below
- ligands: float32 [32768, 128], P(('sections', 'tx')), parts along dimension 0, may hold values from 0.1 to 10
- receptors: float32 [32768, 128], P(('sections', 'tx')), parts along dimension 0, may hold values from 0.1 to 10
- lig_of_pair: int32 [128], replicated, may hold values from 0 to 127
- rec_of_pair: int32 [128], replicated, may hold values from 0 to 127
Outputs:
- received: float32 [32768, 128], P(('sections', 'tx')), parts along dimension 0
The draws below stay inside these ranges and needn't reach their ends.
There are 2 independent parts, one for each index of `sections`. The reference program is written for one: setup_inputs(seed, part) draws one part's arguments, and reference() takes and returns one part's arrays. A program takes and returns all parts, laid end to end along the dimension named above; an argument that names none is the same for every part. Nothing has to cross between parts.
Inputs may be any that keep to these rules, and one draw needn't show every extreme that they name: `positions`: cell slot r has its first coordinate in [r // 128, r // 128 + 1) and its second in [0, 32). `counts`: the live cells of a block are its first slots; the last block is full in every draw.
All inputs are finite; a program needn't handle non-finite values.
Results may differ from the reference program's by a relative error of at most 0.00022.
Values sent between devices are 32-bit elements; how exact they have to be, the bound alone decides.
A program may use at most 64 MiB of HBM per device.

```python
import math
import jax
import jax.numpy as jnp
from jax import lax

BLK = 128
HB = 2
P_SIZE = 128
NLIG = 128
NREC = 128
ITERS = 3
CELLS = 16384
BLOCKS = 128


def draw_positions(key, part):
    key = jax.random.fold_in(key, 3)
    uniform = jax.random.uniform(key, (2, CELLS), jnp.float32)
    across = (jnp.arange(CELLS) // BLK).astype(jnp.float32) + 0.999 * uniform[0]
    along = 32.0 * uniform[1]
    return jnp.stack([across, along], 0)


def draw_counts(key, part):
    key = jax.random.fold_in(key, 7)
    block_index = jnp.arange(BLOCKS)
    baseline = 40 + 88 * block_index // max(BLOCKS - 1, 1)
    jitter = jax.random.randint(key, (BLOCKS,), -16, 17)
    clipped = jnp.clip(baseline + jitter, 1, BLK)
    return jnp.where(block_index == BLOCKS - 1, BLK, clipped).astype(jnp.int32)


def plant(values, rng, least, high):
    dims = values.shape
    index_at = [jax.random.randint(jax.random.fold_in(rng, axis), (), 0, dims[axis]) for axis in range(len(dims))]
    values = values.at[tuple(index_at)].set(least)
    longest = dims.index(max(dims))
    index_at[longest] = (index_at[longest] + 1) % dims[longest]
    return values.at[tuple(index_at)].set(high)


def levels(stream_key, extent, cuts, smallest, high):
    factor_of = 1.0
    for position, shards_of in cuts:
        steps = jax.random.uniform(jax.random.fold_in(jax.random.fold_in(stream_key, 6), position), (shards_of,), jnp.float32, smallest / len(cuts), high / len(cuts))
        factor_of = factor_of * jnp.repeat(jnp.exp(steps), extent[position] // shards_of).reshape((-1,) + (1,) * (len(extent) - 1 - position))
    return factor_of


def setup_inputs(seed: int = 0, part: int = 0) -> dict:
    splits = jax.random.split(jax.random.key(seed), 7)
    part_keys = jax.random.split(jax.random.fold_in(splits[6], part), 7)
    positions = draw_positions(jax.random.fold_in(jax.random.fold_in(splits[6], part), 71), part)
    counts = draw_counts(jax.random.fold_in(jax.random.fold_in(splits[6], part), 71), part)
    ligands = jnp.clip(jnp.exp(math.log(10.0) - 4.6051702 * jax.random.uniform(part_keys[2], (CELLS, NLIG), jnp.float32) ** levels(part_keys[2], (CELLS, NLIG), ((0, 16),), -0.2, 0.2)), 0.1, 10.0)
    receptors = jnp.clip(jnp.exp(math.log(10.0) - 4.6051702 * jax.random.uniform(part_keys[3], (CELLS, NREC), jnp.float32) ** levels(part_keys[3], (CELLS, NREC), ((0, 16),), -0.2, 0.2)), 0.1, 10.0)
    lig_of_pair = plant(jax.random.randint(splits[4], (P_SIZE,), 0, NLIG), jax.random.fold_in(splits[4], 1), 0, NLIG - 1).astype(jnp.int32)
    rec_of_pair = plant(jax.random.randint(splits[5], (P_SIZE,), 0, NREC), jax.random.fold_in(splits[5], 1), 0, NREC - 1).astype(jnp.int32)
    return {"positions": positions, "counts": counts, "ligands": ligands, "receptors": receptors, "lig_of_pair": lig_of_pair, "rec_of_pair": rec_of_pair}


entropy = 0.5
relaxation = 1.0


def pair_kernel(row_x, row_y, col_x, col_y):
    radius = float(HB)
    scaled_sq = (jnp.square(row_x - col_x) + jnp.square(row_y - col_y)) / (radius * radius)
    tapered = jnp.square(jnp.maximum(1.0 - scaled_sq, 0.0))
    return tapered * jnp.exp(-scaled_sq / entropy)


def band_apply(positions, values):
    rim_rows = HB * BLK
    span_rows = (2 * HB + 1) * BLK
    padded_pos = jnp.pad(positions, ((0, 0), (rim_rows, rim_rows)))
    padded_val = jnp.pad(values, ((rim_rows, rim_rows), (0, 0)))

    def one_block(block_index):
        offset = block_index * BLK
        own_pos = lax.dynamic_slice_in_dim(positions, offset, BLK, 1)
        near_pos = lax.dynamic_slice_in_dim(padded_pos, offset, span_rows, 1)
        near_val = lax.dynamic_slice_in_dim(padded_val, offset, span_rows, 0)
        kernel_block = pair_kernel(own_pos[0][:, None], own_pos[1][:, None], near_pos[0][None, :], near_pos[1][None, :])
        return jnp.dot(kernel_block, near_val, precision=lax.Precision.HIGHEST, preferred_element_type=jnp.float32)

    result = lax.map(one_block, jnp.arange(CELLS // BLK, dtype=jnp.int32))
    return result.reshape(CELLS, values.shape[1])


def reference(positions, counts, ligands, receptors, lig_of_pair, rec_of_pair):
    slot_pos = jnp.arange(CELLS, dtype=jnp.int32) % BLK
    live_mask = (slot_pos < jnp.repeat(counts, BLK)).astype(jnp.float32)[:, None]
    pick_lig = (jnp.arange(NLIG, dtype=jnp.int32)[:, None] == lig_of_pair[None, :]).astype(jnp.float32)
    pick_rec = (jnp.arange(NREC, dtype=jnp.int32)[:, None] == rec_of_pair[None, :]).astype(jnp.float32)
    supply = jnp.dot(ligands, pick_lig, precision=lax.Precision.HIGHEST, preferred_element_type=jnp.float32)
    demand = jnp.dot(receptors, pick_rec, precision=lax.Precision.HIGHEST, preferred_element_type=jnp.float32)
    log_supply = jnp.log(supply)
    log_demand = jnp.log(demand)
    factor = relaxation / (relaxation + entropy)
    recv_pot = jnp.zeros((CELLS, P_SIZE), jnp.float32)
    gathered = jnp.zeros((CELLS, P_SIZE), jnp.float32)
    for rounds in range(ITERS):
        sent_mass = band_apply(positions, live_mask * jnp.exp(recv_pot / entropy))
        send_pot = live_mask * factor * entropy * (log_supply - jnp.log(sent_mass + 1.0 - live_mask))
        gathered = band_apply(positions, live_mask * jnp.exp(send_pot / entropy))
        recv_pot = live_mask * factor * entropy * (log_demand - jnp.log(gathered + 1.0 - live_mask))
    flux_out = live_mask * jnp.exp(recv_pot / entropy) * gathered
    totals = jnp.sum(flux_out, axis=0)
    live_total = jnp.sum(counts.astype(jnp.float32))
    return flux_out * (live_total / totals)[None, :]
```

```python
import functools
import math

import jax
import jax.numpy as jnp
from jax import lax
from jax.experimental import pallas as pl
from jax.experimental.pallas import tpu as pltpu
from jax.sharding import PartitionSpec as P

BLK = 128
HB = 2
ITERS = 3
RIM = HB * BLK
FAR = 1.0e6

entropy = 0.5
relaxation = 1.0
FACTOR = relaxation / (relaxation + entropy)
LOG2E = math.log2(math.e)
POWER = FACTOR * LOG2E
ROUNDS = 2 * ITERS - 1
SETS = 2


def split(x):
    hi = x.astype(jnp.bfloat16)
    lo = (x - hi.astype(jnp.float32)).astype(jnp.bfloat16)
    return hi, lo


def kernel(
    n,
    pos_ref,
    counts_ref,
    lig_of_ref,
    rec_of_ref,
    lig_hbm,
    rec_hbm,
    flux_hbm,
    scale_ref,
    lig,
    rec,
    own,
    rows,
    pos_send,
    pos_recv,
    xj,
    yj,
    live,
    k_hi,
    k_lo,
    logs,
    values,
    send,
    recv,
    flux_t,
    flux,
    sums,
    in_sem,
    out_sem,
    pos_send_sem,
    pos_recv_sem,
    send_sem,
    recv_sem,
    sum_send_sem,
    sum_recv_sem,
):
    cells = pos_ref.shape[1]
    nblock = cells // BLK
    tiles = cells // RIM
    half = logs.shape[1] // SETS
    me = lax.axis_index("tx")
    has = (me > 0, me < n - 1)
    beside = (lax.rem(me + n - 1, n), lax.rem(me + 1, n))

    lig_copy = pltpu.make_async_copy(lig_hbm, lig, in_sem.at[0])
    rec_copy = pltpu.make_async_copy(rec_hbm, rec, in_sem.at[1])
    lig_copy.start()
    rec_copy.start()

    barrier = pltpu.get_barrier_semaphore()

    @pl.loop(1, n)
    def _(d):
        pl.semaphore_signal(
            barrier,
            inc=1,
            device_id={"tx": lax.rem(me + d, n)},
            device_id_type=pl.DeviceIdType.MESH,
        )

    def remote(src, dst, ssem, rsem, to):
        return pltpu.make_async_remote_copy(
            src_ref=src,
            dst_ref=dst,
            send_sem=ssem,
            recv_sem=rsem,
            device_id={"tx": to},
            device_id_type=pl.DeviceIdType.MESH,
        )

    lane = lax.broadcasted_iota(jnp.int32, (1, BLK), 1)
    live_count = jnp.zeros((1, BLK), jnp.float32)
    for b in range(nblock):
        count = counts_ref[b]
        mask = lane < count
        live[:, b * BLK : (b + 1) * BLK] = jnp.where(mask, 1.0, 0.0)
        live_count = live_count + count.astype(jnp.float32)
        x = pos_ref[0:1, b * BLK : (b + 1) * BLK] * (1.0 / HB)
        y = pos_ref[1:2, b * BLK : (b + 1) * BLK] * (1.0 / HB)
        own[b, 0:1, :] = x
        own[b, 1:2, :] = y
        rows[b, 0:1, :] = jnp.where(mask, x, FAR)
        rows[b, 1:2, :] = y
    for b in range(HB):
        pos_send[0, b] = rows[b]
        pos_send[1, b] = rows[nblock - HB + b]

    pl.semaphore_wait(barrier, n - 1)

    def pos_copy(side):
        return remote(
            pos_send.at[side],
            pos_recv.at[1 - side],
            pos_send_sem.at[side],
            pos_recv_sem.at[1 - side],
            beside[side],
        )

    def pos_arrival(side):
        return remote(
            pos_send.at[side],
            pos_recv.at[side],
            pos_send_sem.at[side],
            pos_recv_sem.at[side],
            beside[side],
        )

    for side in range(2):
        pl.when(has[side])(pos_copy(side).start)

    def columns(x_row, y_row, at):
        xj[at : at + BLK, :] = jnp.broadcast_to(x_row, (BLK, BLK)).T
        yj[at : at + BLK, :] = jnp.broadcast_to(y_row, (BLK, BLK)).T

    for b in range(nblock):
        columns(rows[b, 0:1, :], rows[b, 1:2, :], RIM + b * BLK)

    def tile_of(t):
        for q in range(HB):
            xi = own[HB * t + q, 0:1, :]
            yi = own[HB * t + q, 1:2, :]
            for w in range(3 * HB):
                at = (pl.ds(w * BLK, BLK), pl.ds(q * BLK, BLK))
                if abs(w - HB - q) > HB:
                    k_hi[t, at[0], at[1]] = jnp.zeros((BLK, BLK), jnp.bfloat16)
                    k_lo[t, at[0], at[1]] = jnp.zeros((BLK, BLK), jnp.bfloat16)
                    continue
                here = pl.ds(pl.multiple_of(t * RIM + w * BLK, BLK), BLK)
                c = jnp.square(xj[here, :] - xi) + jnp.square(yj[here, :] - yi)
                taper = jnp.square(jnp.maximum(1.0 - c, 0.0))
                hi, lo = split(taper * jnp.exp2(c * (-LOG2E / entropy)))
                k_hi[t, at[0], at[1]] = hi
                k_lo[t, at[0], at[1]] = lo

    lax.fori_loop(1, tiles - 1, lambda t, _: (tile_of(t), 0)[1], 0)

    def log_pairs(which, source, of_ref):
        pick = jnp.where(
            lax.broadcasted_iota(jnp.int32, (BLK, BLK), 0) == of_ref[...], 1.0, 0.0
        )
        pick = pick.T.astype(jnp.bfloat16)
        pick2 = jnp.concatenate([pick, pick], axis=1)

        @pl.loop(0, tiles)
        def _(t):
            here = pl.ds(pl.multiple_of(t * RIM, RIM), RIM)
            x = jnp.concatenate(split(source[here, :]), axis=1)
            picked = lax.dot_general(
                pick2, x, (((1,), (1,)), ((), ())), preferred_element_type=jnp.float32
            )
            logs[which, :, here] = POWER * jnp.log(picked)

    lig_copy.wait()
    log_pairs(0, lig, lig_of_ref)

    far = jnp.full((1, BLK), FAR, jnp.float32)
    for side in range(2):
        at = 0 if side == 0 else RIM + cells

        @pl.when(has[side])
        def _():
            pos_arrival(side).wait_recv()
            for b in range(HB):
                columns(
                    pos_recv[side, b, 0:1, :], pos_recv[side, b, 1:2, :], at + b * BLK
                )

        @pl.when(jnp.logical_not(has[side]))
        def _():
            for b in range(HB):
                columns(far, far, at + b * BLK)

    lax.fori_loop(0, 2, lambda i, _: (tile_of(i * (tiles - 1)), 0)[1], 0)

    for parity in range(2):
        for s in range(SETS):
            for at in (0, RIM + cells):
                values[parity, s, :, at : at + RIM] = jnp.zeros(
                    (2 * half, RIM), jnp.bfloat16
                )

    def copy_out(k, s, side):
        return remote(
            send.at[k, s, side],
            recv.at[k, s, 1 - side],
            send_sem.at[k, s, side],
            recv_sem.at[k, s, 1 - side],
            beside[side],
        )

    def arrival(k, s, side):
        return remote(
            send.at[k, s, side],
            recv.at[k, s, side],
            send_sem.at[k, s, side],
            recv_sem.at[k, s, side],
            beside[side],
        )

    def scaled(which, s, t, mass):
        alive = live[:, t * RIM : (t + 1) * RIM]
        log_have = logs[which, s * half : (s + 1) * half, t * RIM : (t + 1) * RIM]
        return alive * jnp.exp2(log_have - POWER * jnp.log(mass + (1.0 - alive)))

    def keep(parity, s, t, w):
        hi, lo = split(w)
        at = RIM * (t + 1)
        values[parity, s, 0:half, at : at + RIM] = hi
        values[parity, s, half:, at : at + RIM] = lo

    edges = ((0, 0), (1, tiles - 1))

    def start(k, s):
        for side, _ in edges:
            pl.when(has[side])(copy_out(k, s, side).start)

    def first(t):
        ones = jnp.ones((16, 3 * RIM), jnp.bfloat16)
        return jnp.dot(ones, k_hi[t], preferred_element_type=jnp.float32)[0:1, :]

    masses = [first(t) for _, t in edges]
    for s in range(SETS):
        for side, t in edges:
            w = scaled(0, s, t, masses[side])
            send[0, s, side] = w
            keep(0, s, t, w)
        start(0, s)
    for t in range(1, tiles - 1):
        mass = first(t)
        for s in range(SETS):
            keep(0, s, t, scaled(0, s, t, mass))

    rec_copy.wait()
    log_pairs(1, rec, rec_of_ref)

    def arrive(k, parity, s):
        for side, _ in edges:
            at = 0 if side == 0 else RIM + cells

            @pl.when(has[side])
            def _():
                arrival(k, s, side).wait_recv()
                hi, lo = split(recv[k, s, side])
                values[parity, s, 0:half, at : at + RIM] = hi
                values[parity, s, half:, at : at + RIM] = lo

    def mass_of(parity, s, t):
        both = jnp.dot(
            values[parity, s, :, t * RIM : (t + 3) * RIM],
            k_hi[t],
            preferred_element_type=jnp.float32,
        )
        return both[0:half] + both[half:]

    def one_round(k, parity):
        which = 1 - parity
        for s in range(SETS):
            arrive(k, parity, s)
            for side, t in edges:
                w = scaled(which, s, t, mass_of(parity, s, t))
                send[k + 1, s, side] = w
                keep(1 - parity, s, t, w)
            start(k + 1, s)
        for s in range(SETS):
            for t in range(1, tiles - 1):
                keep(1 - parity, s, t, scaled(which, s, t, mass_of(parity, s, t)))

    def two_rounds(i, carry):
        one_round(2 * i, 0)
        one_round(2 * i + 1, 1)
        return carry

    lax.fori_loop(0, (ROUNDS - 1) // 2, two_rounds, 0)

    last = ROUNDS - 1
    parity = last % 2

    def finish(s, t):
        gathered = mass_of(parity, s, t) + jnp.dot(
            values[parity, s, 0:half, t * RIM : (t + 3) * RIM],
            k_lo[t],
            preferred_element_type=jnp.float32,
        )
        flux_t[s * half : (s + 1) * half, t * RIM : (t + 1) * RIM] = (
            scaled(1, s, t, gathered) * gathered
        )

    def turn(t):
        total = jnp.zeros((1, BLK), jnp.float32)
        for b in range(HB * t, HB * (t + 1)):
            out = flux_t[:, b * BLK : (b + 1) * BLK].T
            flux[b * BLK : (b + 1) * BLK, :] = out
            total = total + jnp.sum(out, axis=0, keepdims=True)
        return total

    totals = jnp.zeros((1, BLK), jnp.float32)
    for t in range(1, tiles - 1):
        for s in range(SETS):
            finish(s, t)
        totals = totals + turn(t)
    for s in range(SETS):
        arrive(last, parity, s)
        for _, t in edges:
            finish(s, t)
    for _, t in edges:
        totals = totals + turn(t)

    sums[0, 0:1, :] = totals
    sums[0, 1:2, :] = live_count

    def sum_copy(d):
        return remote(
            sums.at[0],
            sums.at[d],
            sum_send_sem.at[d],
            sum_recv_sem.at[d],
            lax.rem(me + d, n),
        )

    @pl.loop(1, n)
    def _(d):
        sum_copy(d).start()

    out_copy = pltpu.make_async_copy(flux, flux_hbm, out_sem)
    out_copy.start()

    for side in range(2):

        @pl.when(has[side])
        def _():
            pos_copy(side).wait_send()
            for s in range(SETS):
                for k in range(ROUNDS):
                    copy_out(k, s, side).wait_send()

    @pl.loop(1, n)
    def _(d):
        sum_copy(d).wait()

    whole = jnp.sum(sums[...], axis=0)
    scale_ref[0:1, :] = whole[1:2, :] / whole[0:1, :]
    out_copy.wait()


def body(positions, counts, ligands, receptors, lig_of_pair, rec_of_pair):
    n = lax.axis_size("tx")
    cells = positions.shape[1]
    nblock = counts.shape[0]
    tiles = cells // RIM
    pairs = lig_of_pair.shape[0]
    wide = cells + 2 * RIM
    half = pairs // SETS
    f32, bf16 = jnp.float32, jnp.bfloat16
    vmem = pl.BlockSpec(memory_space=pltpu.VMEM)
    smem = pl.BlockSpec(memory_space=pltpu.SMEM)
    hbm = pl.BlockSpec(memory_space=pl.ANY)
    flux, scale = pl.pallas_call(
        functools.partial(kernel, n),
        out_shape=(
            jax.ShapeDtypeStruct((cells, pairs), f32),
            jax.ShapeDtypeStruct((1, pairs), f32),
        ),
        in_specs=[vmem, smem, vmem, vmem, hbm, hbm],
        out_specs=(hbm, vmem),
        scratch_shapes=[
            pltpu.VMEM(ligands.shape, f32),
            pltpu.VMEM(receptors.shape, f32),
            pltpu.VMEM((nblock, 8, BLK), f32),
            pltpu.VMEM((nblock, 8, BLK), f32),
            pltpu.VMEM((2, HB, 8, BLK), f32),
            pltpu.VMEM((2, HB, 8, BLK), f32),
            pltpu.VMEM((wide, BLK), f32),
            pltpu.VMEM((wide, BLK), f32),
            pltpu.VMEM((1, cells), f32),
            pltpu.VMEM((tiles, 3 * RIM, RIM), bf16),
            pltpu.VMEM((tiles, 3 * RIM, RIM), bf16),
            pltpu.VMEM((2, pairs, cells), f32),
            pltpu.VMEM((2, SETS, 2 * half, wide), bf16),
            pltpu.VMEM((ROUNDS, SETS, 2, half, RIM), f32),
            pltpu.VMEM((ROUNDS, SETS, 2, half, RIM), f32),
            pltpu.VMEM((pairs, cells), f32),
            pltpu.VMEM((cells, pairs), f32),
            pltpu.VMEM((n, 2, BLK), f32),
            pltpu.SemaphoreType.DMA((2,)),
            pltpu.SemaphoreType.DMA,
            pltpu.SemaphoreType.DMA((2,)),
            pltpu.SemaphoreType.DMA((2,)),
            pltpu.SemaphoreType.DMA((ROUNDS, SETS, 2)),
            pltpu.SemaphoreType.DMA((ROUNDS, SETS, 2)),
            pltpu.SemaphoreType.DMA((n,)),
            pltpu.SemaphoreType.DMA((n,)),
        ],
        compiler_params=pltpu.CompilerParams(
            collective_id=0, has_side_effects=True, vmem_limit_bytes=32 * 1024 * 1024
        ),
    )(
        positions,
        counts,
        lig_of_pair.reshape(1, pairs),
        rec_of_pair.reshape(1, pairs),
        ligands,
        receptors,
    )
    return flux * scale


def solution(mesh):
    in_specs = (
        P(None, ("sections", "tx")),
        P(("sections", "tx")),
        P(("sections", "tx"), None),
        P(("sections", "tx"), None),
        P(),
        P(),
    )
    out_specs = P(("sections", "tx"), None)
    return jax.shard_map(body, mesh=mesh, in_specs=in_specs, out_specs=out_specs, check_vma=False)
```

```python
import functools
import math

import jax
import jax.numpy as jnp
from jax import lax
from jax.experimental import pallas as pl
from jax.experimental.pallas import tpu as pltpu
from jax.sharding import PartitionSpec as P

BLK = 128
HB = 2
ITERS = 3
RIM = HB * BLK
FAR = 1.0e6

entropy = 0.5
relaxation = 1.0
FACTOR = relaxation / (relaxation + entropy)
LOG2E = math.log2(math.e)
POWER = FACTOR * LOG2E
ROUNDS = 2 * ITERS - 1
SETS = 2


def split(x):
    hi = x.astype(jnp.bfloat16)
    lo = (x - hi.astype(jnp.float32)).astype(jnp.bfloat16)
    return hi, lo


def kernel(
    n,
    pos_hbm,
    counts_hbm,
    lig_of_hbm,
    rec_of_hbm,
    lig_hbm,
    rec_hbm,
    flux_hbm,
    scale_ref,
    pos_ref,
    counts_ref,
    lig_of_ref,
    rec_of_ref,
    lig,
    rec,
    own,
    rows,
    pos_send,
    pos_recv,
    xj,
    yj,
    live,
    k_hi,
    k_lo,
    logs,
    values,
    send,
    recv,
    flux_t,
    flux,
    sums,
    in_sem,
    out_sem,
    pos_send_sem,
    pos_recv_sem,
    send_sem,
    recv_sem,
    sum_send_sem,
    sum_recv_sem,
):
    cells = pos_hbm.shape[1]
    nblock = cells // BLK
    tiles = cells // RIM
    half = logs.shape[1] // SETS
    me = lax.axis_index("tx")
    has = (me > 0, me < n - 1)
    beside = (lax.rem(me + n - 1, n), lax.rem(me + 1, n))

    counts_copy = pltpu.make_async_copy(counts_hbm, counts_ref, in_sem.at[0])
    pos_copy_in = pltpu.make_async_copy(pos_hbm, pos_ref, in_sem.at[1])
    lig_of_copy = pltpu.make_async_copy(lig_of_hbm, lig_of_ref, in_sem.at[2])
    rec_of_copy = pltpu.make_async_copy(rec_of_hbm, rec_of_ref, in_sem.at[3])
    lig_copy = pltpu.make_async_copy(lig_hbm, lig, in_sem.at[4])
    rec_copy = pltpu.make_async_copy(rec_hbm, rec, in_sem.at[5])
    counts_copy.start()
    pos_copy_in.start()
    lig_of_copy.start()
    rec_of_copy.start()
    lig_copy.start()
    rec_copy.start()

    barrier = pltpu.get_barrier_semaphore()

    @pl.loop(1, n)
    def _(d):
        pl.semaphore_signal(
            barrier,
            inc=1,
            device_id={"tx": lax.rem(me + d, n)},
            device_id_type=pl.DeviceIdType.MESH,
        )

    def remote(src, dst, ssem, rsem, to):
        return pltpu.make_async_remote_copy(
            src_ref=src,
            dst_ref=dst,
            send_sem=ssem,
            recv_sem=rsem,
            device_id={"tx": to},
            device_id_type=pl.DeviceIdType.MESH,
        )

    counts_copy.wait()
    pos_copy_in.wait()
    lane = lax.broadcasted_iota(jnp.int32, (1, BLK), 1)
    live_count = jnp.zeros((1, BLK), jnp.float32)
    for b in range(nblock):
        count = counts_ref[b]
        mask = lane < count
        live[:, b * BLK : (b + 1) * BLK] = jnp.where(mask, 1.0, 0.0)
        live_count = live_count + count.astype(jnp.float32)
        x = pos_ref[0:1, b * BLK : (b + 1) * BLK] * (1.0 / HB)
        y = pos_ref[1:2, b * BLK : (b + 1) * BLK] * (1.0 / HB)
        own[b, 0:1, :] = x
        own[b, 1:2, :] = y
        rows[b, 0:1, :] = jnp.where(mask, x, FAR)
        rows[b, 1:2, :] = y
    for b in range(HB):
        pos_send[0, b] = rows[b]
        pos_send[1, b] = rows[nblock - HB + b]

    pl.semaphore_wait(barrier, n - 1)

    def pos_copy(side):
        return remote(
            pos_send.at[side],
            pos_recv.at[1 - side],
            pos_send_sem.at[side],
            pos_recv_sem.at[1 - side],
            beside[side],
        )

    def pos_arrival(side):
        return remote(
            pos_send.at[side],
            pos_recv.at[side],
            pos_send_sem.at[side],
            pos_recv_sem.at[side],
            beside[side],
        )

    for side in range(2):
        pl.when(has[side])(pos_copy(side).start)

    def columns(x_row, y_row, at):
        xj[at : at + BLK, :] = jnp.broadcast_to(x_row, (BLK, BLK)).T
        yj[at : at + BLK, :] = jnp.broadcast_to(y_row, (BLK, BLK)).T

    for b in range(nblock):
        columns(rows[b, 0:1, :], rows[b, 1:2, :], RIM + b * BLK)

    def tile_of(t):
        for q in range(HB):
            xi = own[HB * t + q, 0:1, :]
            yi = own[HB * t + q, 1:2, :]
            for w in range(3 * HB):
                at = (pl.ds(w * BLK, BLK), pl.ds(q * BLK, BLK))
                if abs(w - HB - q) > HB:
                    k_hi[t, at[0], at[1]] = jnp.zeros((BLK, BLK), jnp.bfloat16)
                    k_lo[t, at[0], at[1]] = jnp.zeros((BLK, BLK), jnp.bfloat16)
                    continue
                here = pl.ds(pl.multiple_of(t * RIM + w * BLK, BLK), BLK)
                c = jnp.square(xj[here, :] - xi) + jnp.square(yj[here, :] - yi)
                taper = jnp.square(jnp.maximum(1.0 - c, 0.0))
                hi, lo = split(taper * jnp.exp2(c * (-LOG2E / entropy)))
                k_hi[t, at[0], at[1]] = hi
                k_lo[t, at[0], at[1]] = lo

    lax.fori_loop(1, tiles - 1, lambda t, _: (tile_of(t), 0)[1], 0)

    def log_pairs(which, source, of_ref):
        pick = jnp.where(
            lax.broadcasted_iota(jnp.int32, (BLK, BLK), 0) == of_ref[...], 1.0, 0.0
        )
        pick = pick.T.astype(jnp.bfloat16)
        pick2 = jnp.concatenate([pick, pick], axis=1)

        @pl.loop(0, tiles)
        def _(t):
            here = pl.ds(pl.multiple_of(t * RIM, RIM), RIM)
            x = jnp.concatenate(split(source[here, :]), axis=1)
            picked = lax.dot_general(
                pick2, x, (((1,), (1,)), ((), ())), preferred_element_type=jnp.float32
            )
            logs[which, :, here] = POWER * jnp.log(picked)

    lig_of_copy.wait()
    lig_copy.wait()
    log_pairs(0, lig, lig_of_ref)

    far = jnp.full((1, BLK), FAR, jnp.float32)
    for side in range(2):
        at = 0 if side == 0 else RIM + cells

        @pl.when(has[side])
        def _():
            pos_arrival(side).wait_recv()
            for b in range(HB):
                columns(
                    pos_recv[side, b, 0:1, :], pos_recv[side, b, 1:2, :], at + b * BLK
                )

        @pl.when(jnp.logical_not(has[side]))
        def _():
            for b in range(HB):
                columns(far, far, at + b * BLK)

    lax.fori_loop(0, 2, lambda i, _: (tile_of(i * (tiles - 1)), 0)[1], 0)

    for parity in range(2):
        for s in range(SETS):
            for at in (0, RIM + cells):
                values[parity, s, :, at : at + RIM] = jnp.zeros(
                    (2 * half, RIM), jnp.bfloat16
                )

    def copy_out(k, s, side):
        return remote(
            send.at[k, s, side],
            recv.at[k, s, 1 - side],
            send_sem.at[k, s, side],
            recv_sem.at[k, s, 1 - side],
            beside[side],
        )

    def arrival(k, s, side):
        return remote(
            send.at[k, s, side],
            recv.at[k, s, side],
            send_sem.at[k, s, side],
            recv_sem.at[k, s, side],
            beside[side],
        )

    def scaled(which, s, t, mass):
        alive = live[:, t * RIM : (t + 1) * RIM]
        log_have = logs[which, s * half : (s + 1) * half, t * RIM : (t + 1) * RIM]
        return alive * jnp.exp2(log_have - POWER * jnp.log(mass + (1.0 - alive)))

    def keep(parity, s, t, w):
        hi, lo = split(w)
        at = RIM * (t + 1)
        values[parity, s, 0:half, at : at + RIM] = hi
        values[parity, s, half:, at : at + RIM] = lo

    edges = ((0, 0), (1, tiles - 1))

    def start(k, s):
        for side, _ in edges:
            pl.when(has[side])(copy_out(k, s, side).start)

    def first(t):
        ones = jnp.ones((16, 3 * RIM), jnp.bfloat16)
        return jnp.dot(ones, k_hi[t], preferred_element_type=jnp.float32)[0:1, :]

    masses = [first(t) for _, t in edges]
    for s in range(SETS):
        for side, t in edges:
            w = scaled(0, s, t, masses[side])
            send[0, s, side] = w
            keep(0, s, t, w)
        start(0, s)
    for t in range(1, tiles - 1):
        mass = first(t)
        for s in range(SETS):
            keep(0, s, t, scaled(0, s, t, mass))

    rec_of_copy.wait()
    rec_copy.wait()
    log_pairs(1, rec, rec_of_ref)

    def arrive(k, parity, s):
        for side, _ in edges:
            at = 0 if side == 0 else RIM + cells

            @pl.when(has[side])
            def _():
                arrival(k, s, side).wait_recv()
                hi, lo = split(recv[k, s, side])
                values[parity, s, 0:half, at : at + RIM] = hi
                values[parity, s, half:, at : at + RIM] = lo

    def mass_of(parity, s, t):
        both = jnp.dot(
            values[parity, s, :, t * RIM : (t + 3) * RIM],
            k_hi[t],
            preferred_element_type=jnp.float32,
        )
        return both[0:half] + both[half:]

    def one_round(k, parity):
        which = 1 - parity
        for s in range(SETS):
            arrive(k, parity, s)
            for side, t in edges:
                w = scaled(which, s, t, mass_of(parity, s, t))
                send[k + 1, s, side] = w
                keep(1 - parity, s, t, w)
            start(k + 1, s)
        for s in range(SETS):
            for t in range(1, tiles - 1):
                keep(1 - parity, s, t, scaled(which, s, t, mass_of(parity, s, t)))

    def two_rounds(i, carry):
        one_round(2 * i, 0)
        one_round(2 * i + 1, 1)
        return carry

    lax.fori_loop(0, (ROUNDS - 1) // 2, two_rounds, 0)

    last = ROUNDS - 1
    parity = last % 2

    def finish(s, t):
        gathered = mass_of(parity, s, t) + jnp.dot(
            values[parity, s, 0:half, t * RIM : (t + 3) * RIM],
            k_lo[t],
            preferred_element_type=jnp.float32,
        )
        flux_t[s * half : (s + 1) * half, t * RIM : (t + 1) * RIM] = (
            scaled(1, s, t, gathered) * gathered
        )

    def turn(t):
        total = jnp.zeros((1, BLK), jnp.float32)
        for b in range(HB * t, HB * (t + 1)):
            out = flux_t[:, b * BLK : (b + 1) * BLK].T
            flux[b * BLK : (b + 1) * BLK, :] = out
            total = total + jnp.sum(out, axis=0, keepdims=True)
        return total

    totals = jnp.zeros((1, BLK), jnp.float32)
    for t in range(1, tiles - 1):
        for s in range(SETS):
            finish(s, t)
        totals = totals + turn(t)
    for s in range(SETS):
        arrive(last, parity, s)
        for _, t in edges:
            finish(s, t)
    for _, t in edges:
        totals = totals + turn(t)

    sums[0, 0:1, :] = totals
    sums[0, 1:2, :] = live_count

    def sum_copy(d):
        return remote(
            sums.at[0],
            sums.at[d],
            sum_send_sem.at[d],
            sum_recv_sem.at[d],
            lax.rem(me + d, n),
        )

    @pl.loop(1, n)
    def _(d):
        sum_copy(d).start()

    out_copy = pltpu.make_async_copy(flux, flux_hbm, out_sem)
    out_copy.start()

    for side in range(2):

        @pl.when(has[side])
        def _():
            pos_copy(side).wait_send()
            for s in range(SETS):
                for k in range(ROUNDS):
                    copy_out(k, s, side).wait_send()

    @pl.loop(1, n)
    def _(d):
        sum_copy(d).wait()

    whole = jnp.sum(sums[...], axis=0)
    scale_ref[0:1, :] = whole[1:2, :] / whole[0:1, :]
    out_copy.wait()


def body(positions, counts, ligands, receptors, lig_of_pair, rec_of_pair):
    n = lax.axis_size("tx")
    cells = positions.shape[1]
    nblock = counts.shape[0]
    tiles = cells // RIM
    pairs = lig_of_pair.shape[0]
    wide = cells + 2 * RIM
    half = pairs // SETS
    f32, bf16 = jnp.float32, jnp.bfloat16
    vmem = pl.BlockSpec(memory_space=pltpu.VMEM)
    smem = pl.BlockSpec(memory_space=pltpu.SMEM)
    hbm = pl.BlockSpec(memory_space=pltpu.HBM)
    flux, scale = pl.pallas_call(
        functools.partial(kernel, n),
        out_shape=(
            jax.ShapeDtypeStruct((cells, pairs), f32),
            jax.ShapeDtypeStruct((1, pairs), f32),
        ),
        in_specs=[hbm] * 6,
        out_specs=(hbm, vmem),
        scratch_shapes=[
            pltpu.VMEM(positions.shape, f32),
            pltpu.SMEM(counts.shape, jnp.int32),
            pltpu.VMEM((1, pairs), jnp.int32),
            pltpu.VMEM((1, pairs), jnp.int32),
            pltpu.VMEM(ligands.shape, f32),
            pltpu.VMEM(receptors.shape, f32),
            pltpu.VMEM((nblock, 8, BLK), f32),
            pltpu.VMEM((nblock, 8, BLK), f32),
            pltpu.VMEM((2, HB, 8, BLK), f32),
            pltpu.VMEM((2, HB, 8, BLK), f32),
            pltpu.VMEM((wide, BLK), f32),
            pltpu.VMEM((wide, BLK), f32),
            pltpu.VMEM((1, cells), f32),
            pltpu.VMEM((tiles, 3 * RIM, RIM), bf16),
            pltpu.VMEM((tiles, 3 * RIM, RIM), bf16),
            pltpu.VMEM((2, pairs, cells), f32),
            pltpu.VMEM((2, SETS, 2 * half, wide), bf16),
            pltpu.VMEM((ROUNDS, SETS, 2, half, RIM), f32),
            pltpu.VMEM((ROUNDS, SETS, 2, half, RIM), f32),
            pltpu.VMEM((pairs, cells), f32),
            pltpu.VMEM((cells, pairs), f32),
            pltpu.VMEM((n, 2, BLK), f32),
            pltpu.SemaphoreType.DMA((6,)),
            pltpu.SemaphoreType.DMA,
            pltpu.SemaphoreType.DMA((2,)),
            pltpu.SemaphoreType.DMA((2,)),
            pltpu.SemaphoreType.DMA((ROUNDS, SETS, 2)),
            pltpu.SemaphoreType.DMA((ROUNDS, SETS, 2)),
            pltpu.SemaphoreType.DMA((n,)),
            pltpu.SemaphoreType.DMA((n,)),
        ],
        compiler_params=pltpu.CompilerParams(
            collective_id=0, has_side_effects=True
        ),
    )(
        positions,
        counts,
        lig_of_pair.reshape(1, pairs),
        rec_of_pair.reshape(1, pairs),
        ligands,
        receptors,
    )
    return flux * scale


def solution(mesh):
    in_specs = (
        P(None, ("sections", "tx")),
        P(("sections", "tx")),
        P(("sections", "tx"), None),
        P(("sections", "tx"), None),
        P(),
        P(),
    )
    out_specs = P(("sections", "tx"), None)
    return jax.shard_map(body, mesh=mesh, in_specs=in_specs, out_specs=out_specs, check_vma=False)
```

```python
import functools
import math

import jax
import jax.numpy as jnp
from jax import lax
from jax.experimental import pallas as pl
from jax.experimental.pallas import tpu as pltpu
from jax.sharding import PartitionSpec as P

BLK = 128
HB = 2
ITERS = 3
RIM = HB * BLK
FAR = 1.0e6

entropy = 0.5
relaxation = 1.0
FACTOR = relaxation / (relaxation + entropy)
LOG2E = math.log2(math.e)
POWER = FACTOR * LOG2E
ROUNDS = ITERS - 1
REACH = 2 * HB
WIDE = REACH * BLK
SETS = 2


def split(x):
    hi = x.astype(jnp.bfloat16)
    lo = (x - hi.astype(jnp.float32)).astype(jnp.bfloat16)
    return hi, lo


def kernel(
    n,
    pos_hbm,
    counts_hbm,
    lig_of_hbm,
    rec_of_hbm,
    lig_hbm,
    rec_hbm,
    flux_hbm,
    scale_ref,
    pos_ref,
    counts_ref,
    lig_of_ref,
    rec_of_ref,
    lig,
    rec,
    own,
    rows,
    pos_send,
    pos_recv,
    xj,
    yj,
    live,
    k_hi,
    k_lo,
    logs,
    values,
    send,
    recv,
    flux_t,
    flux,
    sums,
    in_sem,
    out_sem,
    pos_send_sem,
    pos_recv_sem,
    lig_send_sem,
    lig_recv_sem,
    send_sem,
    recv_sem,
    sum_send_sem,
    sum_recv_sem,
):
    cells = pos_hbm.shape[1]
    nblock = cells // BLK
    tiles = cells // RIM
    half = logs.shape[1] // SETS
    me = lax.axis_index("tx")
    has = (me > 0, me < n - 1)
    beside = (lax.rem(me + n - 1, n), lax.rem(me + 1, n))

    counts_copy = pltpu.make_async_copy(counts_hbm, counts_ref, in_sem.at[0])
    pos_copy_in = pltpu.make_async_copy(pos_hbm, pos_ref, in_sem.at[1])
    lig_of_copy = pltpu.make_async_copy(lig_of_hbm, lig_of_ref, in_sem.at[2])
    rec_of_copy = pltpu.make_async_copy(rec_of_hbm, rec_of_ref, in_sem.at[3])
    lig_copy = pltpu.make_async_copy(
        lig_hbm, lig.at[pl.ds(RIM, cells)], in_sem.at[4]
    )
    rec_copy = pltpu.make_async_copy(rec_hbm, rec, in_sem.at[5])
    counts_copy.start()
    pos_copy_in.start()
    lig_of_copy.start()
    rec_of_copy.start()
    lig_copy.start()
    rec_copy.start()

    barrier = pltpu.get_barrier_semaphore()

    @pl.loop(1, n)
    def _(d):
        pl.semaphore_signal(
            barrier,
            inc=1,
            device_id={"tx": lax.rem(me + d, n)},
            device_id_type=pl.DeviceIdType.MESH,
        )

    def remote(src, dst, ssem, rsem, to):
        return pltpu.make_async_remote_copy(
            src_ref=src,
            dst_ref=dst,
            send_sem=ssem,
            recv_sem=rsem,
            device_id={"tx": to},
            device_id_type=pl.DeviceIdType.MESH,
        )

    counts_copy.wait()
    pos_copy_in.wait()
    lane = lax.broadcasted_iota(jnp.int32, (1, BLK), 1)
    live_count = jnp.zeros((1, BLK), jnp.float32)
    for b in range(nblock):
        count = counts_ref[b]
        mask = lane < count
        live[:, RIM + b * BLK : RIM + (b + 1) * BLK] = jnp.where(mask, 1.0, 0.0)
        live_count = live_count + count.astype(jnp.float32)
        x = pos_ref[0:1, b * BLK : (b + 1) * BLK] * (1.0 / HB)
        y = pos_ref[1:2, b * BLK : (b + 1) * BLK] * (1.0 / HB)
        own[HB + b, 0:1, :] = x
        own[HB + b, 1:2, :] = y
        rows[b, 0:1, :] = jnp.where(mask, x, FAR)
        rows[b, 1:2, :] = y
    for b in range(REACH):
        pos_send[0, b] = rows[b]
        pos_send[1, b] = rows[nblock - REACH + b]

    pl.semaphore_wait(barrier, n - 1)

    def pos_copy(side):
        return remote(
            pos_send.at[side],
            pos_recv.at[1 - side],
            pos_send_sem.at[side],
            pos_recv_sem.at[1 - side],
            beside[side],
        )

    def pos_arrival(side):
        return remote(
            pos_send.at[side],
            pos_recv.at[side],
            pos_send_sem.at[side],
            pos_recv_sem.at[side],
            beside[side],
        )

    ends = (0, RIM + cells)

    def lig_out(side):
        return remote(
            lig_hbm.at[pl.ds(0 if side == 0 else cells - RIM, RIM)],
            lig.at[pl.ds(ends[1 - side], RIM)],
            lig_send_sem.at[side],
            lig_recv_sem.at[1 - side],
            beside[side],
        )

    def lig_arrival(side):
        return remote(
            lig_hbm.at[pl.ds(0 if side == 0 else cells - RIM, RIM)],
            lig.at[pl.ds(ends[side], RIM)],
            lig_send_sem.at[side],
            lig_recv_sem.at[side],
            beside[side],
        )

    for side in range(2):
        pl.when(has[side])(pos_copy(side).start)
    for side in range(2):
        pl.when(has[side])(lig_out(side).start)

    def columns(x_row, y_row, at):
        xj[at : at + BLK, :] = jnp.broadcast_to(x_row, (BLK, BLK)).T
        yj[at : at + BLK, :] = jnp.broadcast_to(y_row, (BLK, BLK)).T

    for b in range(nblock):
        columns(rows[b, 0:1, :], rows[b, 1:2, :], WIDE + b * BLK)

    def tile_of(t):
        for q in range(HB):
            xi = own[HB * t + q, 0:1, :]
            yi = own[HB * t + q, 1:2, :]
            for w in range(3 * HB):
                at = (pl.ds(w * BLK, BLK), pl.ds(q * BLK, BLK))
                if abs(w - HB - q) > HB:
                    k_hi[t, at[0], at[1]] = jnp.zeros((BLK, BLK), jnp.bfloat16)
                    k_lo[t, at[0], at[1]] = jnp.zeros((BLK, BLK), jnp.bfloat16)
                    continue
                here = pl.ds(pl.multiple_of(t * RIM + w * BLK, BLK), BLK)
                c = jnp.square(xj[here, :] - xi) + jnp.square(yj[here, :] - yi)
                taper = jnp.square(jnp.maximum(1.0 - c, 0.0))
                hi, lo = split(taper * jnp.exp2(c * (-LOG2E / entropy)))
                k_hi[t, at[0], at[1]] = hi
                k_lo[t, at[0], at[1]] = lo

    lax.fori_loop(2, tiles, lambda t, _: (tile_of(t), 0)[1], 0)

    def log_pairs(which, source, of_ref, at, count):
        pick = jnp.where(
            lax.broadcasted_iota(jnp.int32, (BLK, BLK), 0) == of_ref[...], 1.0, 0.0
        )
        pick = pick.T.astype(jnp.bfloat16)
        pick2 = jnp.concatenate([pick, pick], axis=1)

        @pl.loop(0, count)
        def _(t):
            here = pl.ds(pl.multiple_of(t * RIM, RIM), RIM)
            there = pl.ds(pl.multiple_of(t * RIM + at, RIM), RIM)
            x = jnp.concatenate(split(source[here, :]), axis=1)
            picked = lax.dot_general(
                pick2, x, (((1,), (1,)), ((), ())), preferred_element_type=jnp.float32
            )
            logs[which, :, there] = POWER * jnp.log(picked)

    rec_of_copy.wait()
    rec_copy.wait()
    log_pairs(1, rec, rec_of_ref, RIM, tiles)

    for side in range(2):
        edge = 0 if side == 0 else WIDE + cells
        inner = HB if side == 0 else 0

        @pl.when(has[side])
        def _():
            pos_arrival(side).wait_recv()

        @pl.when(jnp.logical_not(has[side]))
        def _():
            pos_recv[side] = jnp.full((REACH, 8, BLK), FAR, jnp.float32)
            lig[ends[side] : ends[side] + RIM, :] = jnp.ones((RIM, BLK), jnp.float32)

        for b in range(REACH):
            columns(
                pos_recv[side, b, 0:1, :], pos_recv[side, b, 1:2, :], edge + b * BLK
            )
        for b in range(HB):
            x = pos_recv[side, inner + b, 0:1, :]
            own[side * (HB + nblock) + b, 0:1, :] = x
            own[side * (HB + nblock) + b, 1:2, :] = pos_recv[side, inner + b, 1:2, :]
            at = ends[side] + b * BLK
            live[:, at : at + BLK] = jnp.where(x < 0.5 * FAR, 1.0, 0.0)

    lax.fori_loop(0, 2, lambda i, _: (tile_of(i), 0)[1], 0)
    lax.fori_loop(tiles, tiles + 2, lambda i, _: (tile_of(i), 0)[1], 0)

    lig_of_copy.wait()
    lig_copy.wait()
    for side in range(2):

        @pl.when(has[side])
        def _():
            lig_arrival(side).wait_recv()

    log_pairs(0, lig, lig_of_ref, 0, tiles + 2)

    for s in range(SETS):
        for at in (0, WIDE + cells):
            values[0, s, :, at : at + WIDE] = jnp.zeros((2 * half, WIDE), jnp.bfloat16)

    def copy_out(k, s, side):
        return remote(
            send.at[k, s, side],
            recv.at[k, s, 1 - side],
            send_sem.at[k, s, side],
            recv_sem.at[k, s, 1 - side],
            beside[side],
        )

    def arrival(k, s, side):
        return remote(
            send.at[k, s, side],
            recv.at[k, s, side],
            send_sem.at[k, s, side],
            recv_sem.at[k, s, side],
            beside[side],
        )

    def scaled(which, s, t, mass):
        alive = live[:, t * RIM : (t + 1) * RIM]
        some = pl.ds(pl.multiple_of(s * half, half), half)
        log_have = logs[which, some, t * RIM : (t + 1) * RIM]
        return alive * jnp.exp2(log_have - POWER * jnp.log(mass + (1.0 - alive)))

    def keep(parity, s, t, w):
        hi, lo = split(w)
        at = RIM * (t + 1)
        values[parity, s, 0:half, at : at + RIM] = hi
        values[parity, s, half:, at : at + RIM] = lo

    def start(k, s):
        for side in range(2):
            pl.when(has[side])(copy_out(k, s, side).start)

    for t in range(tiles + 2):
        ones = jnp.ones((16, 3 * RIM), jnp.bfloat16)
        mass = jnp.dot(ones, k_hi[t], preferred_element_type=jnp.float32)[0:1, :]
        for s in range(SETS):
            keep(1, s, t, scaled(0, s, t, mass))

    def arrive(k, s):
        for side in range(2):
            at = 0 if side == 0 else WIDE + cells

            @pl.when(has[side])
            def _():
                arrival(k, s, side).wait_recv()
                hi, lo = split(recv[k, s, side])
                values[0, s, 0:half, at : at + WIDE] = hi
                values[0, s, half:, at : at + WIDE] = lo

    def mass_of(parity, s, t):
        both = jnp.dot(
            values[parity, s, :, t * RIM : (t + 3) * RIM],
            k_hi[t],
            preferred_element_type=jnp.float32,
        )
        return both[0:half] + both[half:]

    def send_side(s, t):
        keep(1, s, t, scaled(0, s, t, mass_of(0, s, t)))

    def receive_side(k, s):
        for t in range(1, tiles + 1):
            w = scaled(1, s, t, mass_of(1, s, t))
            keep(0, s, t, w)
            if t <= 2:
                send[k, s, 0, :, (t - 1) * RIM : t * RIM] = w
            if t > tiles - 2:
                at = (t + 1 - tiles) * RIM
                send[k, s, 1, :, at : at + RIM] = w
        start(k, s)

    def finish(s, t):
        gathered = mass_of(1, s, t) + jnp.dot(
            values[1, s, 0:half, t * RIM : (t + 3) * RIM],
            k_lo[t],
            preferred_element_type=jnp.float32,
        )
        some = pl.ds(pl.multiple_of(s * half, half), half)
        flux_t[some, (t - 1) * RIM : t * RIM] = (
            scaled(1, s, t, gathered) * gathered
        )

    def turn(t):
        total = jnp.zeros((1, BLK), jnp.float32)
        for b in range(HB * t, HB * (t + 1)):
            out = flux_t[:, b * BLK : (b + 1) * BLK].T
            flux[b * BLK : (b + 1) * BLK, :] = out
            total = total + jnp.sum(out, axis=0, keepdims=True)
        return total

    pl.loop(0, SETS)(lambda s: receive_side(0, s))
    for k in range(ROUNDS):

        @pl.loop(0, SETS)
        def _(s):
            for t in range(2, tiles):
                send_side(s, t)

        @pl.loop(0, SETS)
        def _(s):
            arrive(k, s)
            for t in (0, 1, tiles, tiles + 1):
                send_side(s, t)
            if k + 1 < ROUNDS:
                receive_side(k + 1, s)
            else:
                for t in range(1, tiles + 1):
                    finish(s, t)

    totals = jnp.zeros((1, BLK), jnp.float32)
    for t in range(tiles):
        totals = totals + turn(t)

    sums[0, 0:1, :] = totals
    sums[0, 1:2, :] = live_count

    def sum_copy(d):
        return remote(
            sums.at[0],
            sums.at[d],
            sum_send_sem.at[d],
            sum_recv_sem.at[d],
            lax.rem(me + d, n),
        )

    @pl.loop(1, n)
    def _(d):
        sum_copy(d).start()

    out_copy = pltpu.make_async_copy(flux, flux_hbm, out_sem)
    out_copy.start()

    for side in range(2):

        @pl.when(has[side])
        def _():
            pos_copy(side).wait_send()
            lig_out(side).wait_send()
            for s in range(SETS):
                for k in range(ROUNDS):
                    copy_out(k, s, side).wait_send()

    @pl.loop(1, n)
    def _(d):
        sum_copy(d).wait()

    whole = jnp.sum(sums[...], axis=0)
    scale_ref[0:1, :] = whole[1:2, :] / whole[0:1, :]
    out_copy.wait()


def body(positions, counts, ligands, receptors, lig_of_pair, rec_of_pair):
    n = lax.axis_size("tx")
    cells = positions.shape[1]
    nblock = counts.shape[0]
    tiles = cells // RIM
    pairs = lig_of_pair.shape[0]
    inside = cells + 2 * RIM
    wide = cells + 2 * WIDE
    half = pairs // SETS
    f32, bf16 = jnp.float32, jnp.bfloat16
    vmem = pl.BlockSpec(memory_space=pltpu.VMEM)
    smem = pl.BlockSpec(memory_space=pltpu.SMEM)
    hbm = pl.BlockSpec(memory_space=pltpu.HBM)
    flux, scale = pl.pallas_call(
        functools.partial(kernel, n),
        out_shape=(
            jax.ShapeDtypeStruct((cells, pairs), f32),
            jax.ShapeDtypeStruct((1, pairs), f32),
        ),
        in_specs=[hbm] * 6,
        out_specs=(hbm, vmem),
        scratch_shapes=[
            pltpu.VMEM(positions.shape, f32),
            pltpu.SMEM(counts.shape, jnp.int32),
            pltpu.VMEM((1, pairs), jnp.int32),
            pltpu.VMEM((1, pairs), jnp.int32),
            pltpu.VMEM((inside, ligands.shape[1]), f32),
            pltpu.VMEM(receptors.shape, f32),
            pltpu.VMEM((nblock + 2 * HB, 8, BLK), f32),
            pltpu.VMEM((nblock, 8, BLK), f32),
            pltpu.VMEM((2, REACH, 8, BLK), f32),
            pltpu.VMEM((2, REACH, 8, BLK), f32),
            pltpu.VMEM((wide, BLK), f32),
            pltpu.VMEM((wide, BLK), f32),
            pltpu.VMEM((1, inside), f32),
            pltpu.VMEM((tiles + 2, 3 * RIM, RIM), bf16),
            pltpu.VMEM((tiles + 2, 3 * RIM, RIM), bf16),
            pltpu.VMEM((2, pairs, inside), f32),
            pltpu.VMEM((2, SETS, 2 * half, wide), bf16),
            pltpu.VMEM((ROUNDS, SETS, 2, half, WIDE), f32),
            pltpu.VMEM((ROUNDS, SETS, 2, half, WIDE), f32),
            pltpu.VMEM((pairs, cells), f32),
            pltpu.VMEM((cells, pairs), f32),
            pltpu.VMEM((n, 2, BLK), f32),
            pltpu.SemaphoreType.DMA((6,)),
            pltpu.SemaphoreType.DMA,
            pltpu.SemaphoreType.DMA((2,)),
            pltpu.SemaphoreType.DMA((2,)),
            pltpu.SemaphoreType.DMA((2,)),
            pltpu.SemaphoreType.DMA((2,)),
            pltpu.SemaphoreType.DMA((ROUNDS, SETS, 2)),
            pltpu.SemaphoreType.DMA((ROUNDS, SETS, 2)),
            pltpu.SemaphoreType.DMA((n,)),
            pltpu.SemaphoreType.DMA((n,)),
        ],
        compiler_params=pltpu.CompilerParams(
            collective_id=0, has_side_effects=True
        ),
    )(
        positions,
        counts,
        lig_of_pair.reshape(1, pairs),
        rec_of_pair.reshape(1, pairs),
        ligands,
        receptors,
    )
    return flux * scale


def solution(mesh):
    in_specs = (
        P(None, ("sections", "tx")),
        P(("sections", "tx")),
        P(("sections", "tx"), None),
        P(("sections", "tx"), None),
        P(),
        P(),
    )
    out_specs = P(("sections", "tx"), None)
    return jax.shard_map(body, mesh=mesh, in_specs=in_specs, out_specs=out_specs, check_vma=False)
```

```python
import functools
import math

import jax
import jax.numpy as jnp
from jax import lax
from jax.experimental import pallas as pl
from jax.experimental.pallas import tpu as pltpu
from jax.sharding import PartitionSpec as P

BLK = 128
HB = 2
ITERS = 3
RIM = HB * BLK
FAR = 1.0e6

entropy = 0.5
relaxation = 1.0
FACTOR = relaxation / (relaxation + entropy)
LOG2E = math.log2(math.e)
POWER = FACTOR * LOG2E
ROUNDS = ITERS - 1
REACH = 2 * HB
WIDE = REACH * BLK
SETS = 2


def split(x):
    hi = x.astype(jnp.bfloat16)
    lo = (x - hi.astype(jnp.float32)).astype(jnp.bfloat16)
    return hi, lo


def kernel(
    n,
    pos_hbm,
    counts_hbm,
    lig_of_hbm,
    rec_of_hbm,
    lig_hbm,
    rec_hbm,
    flux_hbm,
    scale_ref,
    pos_ref,
    counts_ref,
    lig_of_ref,
    rec_of_ref,
    lig,
    rec,
    own,
    rows,
    pos_send,
    pos_recv,
    xj,
    yj,
    live,
    k_hi,
    k_lo,
    logs,
    values,
    send,
    recv,
    flux_t,
    flux,
    sums,
    in_sem,
    out_sem,
    pos_send_sem,
    pos_recv_sem,
    lig_send_sem,
    lig_recv_sem,
    send_sem,
    recv_sem,
    sum_send_sem,
    sum_recv_sem,
):
    cells = pos_hbm.shape[1]
    nblock = cells // BLK
    tiles = cells // RIM
    half = logs.shape[1] // SETS
    me = lax.axis_index("tx")
    has = (me > 0, me < n - 1)
    beside = (lax.rem(me + n - 1, n), lax.rem(me + 1, n))

    counts_copy = pltpu.make_async_copy(counts_hbm, counts_ref, in_sem.at[0])
    pos_copy_in = pltpu.make_async_copy(pos_hbm, pos_ref, in_sem.at[1])
    lig_of_copy = pltpu.make_async_copy(lig_of_hbm, lig_of_ref, in_sem.at[2])
    rec_of_copy = pltpu.make_async_copy(rec_of_hbm, rec_of_ref, in_sem.at[3])
    lig_copy = pltpu.make_async_copy(
        lig_hbm, lig.at[pl.ds(RIM, cells)], in_sem.at[4]
    )
    rec_copy = pltpu.make_async_copy(rec_hbm, rec, in_sem.at[5])
    counts_copy.start()
    pos_copy_in.start()
    lig_of_copy.start()
    rec_of_copy.start()
    lig_copy.start()
    rec_copy.start()

    barrier = pltpu.get_barrier_semaphore()

    @pl.loop(1, n)
    def _(d):
        pl.semaphore_signal(
            barrier,
            inc=1,
            device_id={"tx": lax.rem(me + d, n)},
            device_id_type=pl.DeviceIdType.MESH,
        )

    def remote(src, dst, ssem, rsem, to):
        return pltpu.make_async_remote_copy(
            src_ref=src,
            dst_ref=dst,
            send_sem=ssem,
            recv_sem=rsem,
            device_id={"tx": to},
            device_id_type=pl.DeviceIdType.MESH,
        )

    counts_copy.wait()
    pos_copy_in.wait()
    lane = lax.broadcasted_iota(jnp.int32, (1, BLK), 1)
    live_count = jnp.zeros((1, BLK), jnp.float32)
    for b in range(nblock):
        count = counts_ref[b]
        mask = lane < count
        live[:, RIM + b * BLK : RIM + (b + 1) * BLK] = jnp.where(mask, 1.0, 0.0)
        live_count = live_count + count.astype(jnp.float32)
        x = pos_ref[0:1, b * BLK : (b + 1) * BLK] * (1.0 / HB)
        y = pos_ref[1:2, b * BLK : (b + 1) * BLK] * (1.0 / HB)
        own[HB + b, 0:1, :] = x
        own[HB + b, 1:2, :] = y
        rows[b, 0:1, :] = jnp.where(mask, x, FAR)
        rows[b, 1:2, :] = y
    for b in range(REACH):
        pos_send[0, b] = rows[b]
        pos_send[1, b] = rows[nblock - REACH + b]

    pl.semaphore_wait(barrier, n - 1)

    def pos_copy(side):
        return remote(
            pos_send.at[side],
            pos_recv.at[1 - side],
            pos_send_sem.at[side],
            pos_recv_sem.at[1 - side],
            beside[side],
        )

    def pos_arrival(side):
        return remote(
            pos_send.at[side],
            pos_recv.at[side],
            pos_send_sem.at[side],
            pos_recv_sem.at[side],
            beside[side],
        )

    ends = (0, RIM + cells)

    def lig_out(side):
        return remote(
            lig_hbm.at[pl.ds(0 if side == 0 else cells - RIM, RIM)],
            lig.at[pl.ds(ends[1 - side], RIM)],
            lig_send_sem.at[side],
            lig_recv_sem.at[1 - side],
            beside[side],
        )

    def lig_arrival(side):
        return remote(
            lig_hbm.at[pl.ds(0 if side == 0 else cells - RIM, RIM)],
            lig.at[pl.ds(ends[side], RIM)],
            lig_send_sem.at[side],
            lig_recv_sem.at[side],
            beside[side],
        )

    for side in range(2):
        pl.when(has[side])(pos_copy(side).start)
    for side in range(2):
        pl.when(has[side])(lig_out(side).start)

    def columns(x_row, y_row, at):
        xj[at : at + BLK, :] = jnp.broadcast_to(x_row, (BLK, BLK)).T
        yj[at : at + BLK, :] = jnp.broadcast_to(y_row, (BLK, BLK)).T

    for b in range(nblock):
        columns(rows[b, 0:1, :], rows[b, 1:2, :], WIDE + b * BLK)

    def tile_of(t):
        for q in range(HB):
            xi = own[HB * t + q, 0:1, :]
            yi = own[HB * t + q, 1:2, :]
            for w in range(3 * HB):
                at = (pl.ds(w * BLK, BLK), pl.ds(q * BLK, BLK))
                if abs(w - HB - q) > HB:
                    k_hi[t, at[0], at[1]] = jnp.zeros((BLK, BLK), jnp.bfloat16)
                    k_lo[t, at[0], at[1]] = jnp.zeros((BLK, BLK), jnp.bfloat16)
                    continue
                here = pl.ds(pl.multiple_of(t * RIM + w * BLK, BLK), BLK)
                c = jnp.square(xj[here, :] - xi) + jnp.square(yj[here, :] - yi)
                taper = jnp.square(jnp.maximum(1.0 - c, 0.0))
                hi, lo = split(taper * jnp.exp2(c * (-LOG2E / entropy)))
                k_hi[t, at[0], at[1]] = hi
                k_lo[t, at[0], at[1]] = lo

    lax.fori_loop(2, tiles, lambda t, _: (tile_of(t), 0)[1], 0)

    def log_pairs(which, source, of_ref, at, count):
        pick = jnp.where(
            lax.broadcasted_iota(jnp.int32, (BLK, BLK), 0) == of_ref[...], 1.0, 0.0
        )
        pick = pick.T.astype(jnp.bfloat16)
        pick2 = jnp.concatenate([pick, pick], axis=1)

        @pl.loop(0, count)
        def _(t):
            here = pl.ds(pl.multiple_of(t * RIM, RIM), RIM)
            there = pl.ds(pl.multiple_of(t * RIM + at, RIM), RIM)
            x = jnp.concatenate(split(source[here, :]), axis=1)
            picked = lax.dot_general(
                pick2, x, (((1,), (1,)), ((), ())), preferred_element_type=jnp.float32
            )
            logs[which, :, there] = POWER * jnp.log(picked)

    rec_of_copy.wait()
    rec_copy.wait()
    log_pairs(1, rec, rec_of_ref, RIM, tiles)

    for side in range(2):
        edge = 0 if side == 0 else WIDE + cells
        inner = HB if side == 0 else 0

        @pl.when(has[side])
        def _():
            pos_arrival(side).wait_recv()

        @pl.when(jnp.logical_not(has[side]))
        def _():
            pos_recv[side] = jnp.full((REACH, 8, BLK), FAR, jnp.float32)
            lig[ends[side] : ends[side] + RIM, :] = jnp.ones((RIM, BLK), jnp.float32)

        for b in range(REACH):
            columns(
                pos_recv[side, b, 0:1, :], pos_recv[side, b, 1:2, :], edge + b * BLK
            )
        for b in range(HB):
            x = pos_recv[side, inner + b, 0:1, :]
            own[side * (HB + nblock) + b, 0:1, :] = x
            own[side * (HB + nblock) + b, 1:2, :] = pos_recv[side, inner + b, 1:2, :]
            at = ends[side] + b * BLK
            live[:, at : at + BLK] = jnp.where(x < 0.5 * FAR, 1.0, 0.0)

    lax.fori_loop(0, 2, lambda i, _: (tile_of(i), 0)[1], 0)
    lax.fori_loop(tiles, tiles + 2, lambda i, _: (tile_of(i), 0)[1], 0)

    lig_of_copy.wait()
    lig_copy.wait()
    for side in range(2):

        @pl.when(has[side])
        def _():
            lig_arrival(side).wait_recv()

    log_pairs(0, lig, lig_of_ref, 0, tiles + 2)

    for s in range(SETS):
        for at in (0, WIDE + cells):
            values[0, s, :, at : at + WIDE] = jnp.zeros((2 * half, WIDE), jnp.bfloat16)

    def copy_out(k, s, side):
        return remote(
            send.at[k, s, side],
            recv.at[k, s, 1 - side],
            send_sem.at[k, s, side],
            recv_sem.at[k, s, 1 - side],
            beside[side],
        )

    def arrival(k, s, side):
        return remote(
            send.at[k, s, side],
            recv.at[k, s, side],
            send_sem.at[k, s, side],
            recv_sem.at[k, s, side],
            beside[side],
        )

    def scaled(which, s, t, mass):
        alive = live[:, t * RIM : (t + 1) * RIM]
        some = pl.ds(pl.multiple_of(s * half, half), half)
        log_have = logs[which, some, t * RIM : (t + 1) * RIM]
        return alive * jnp.exp2(log_have - POWER * jnp.log(mass + (1.0 - alive)))

    def keep(parity, s, t, w):
        hi, lo = split(w)
        at = RIM * (t + 1)
        values[parity, s, 0:half, at : at + RIM] = hi
        values[parity, s, half:, at : at + RIM] = lo

    def start(k, s):
        for side in range(2):
            pl.when(has[side])(copy_out(k, s, side).start)

    for t in range(tiles + 2):
        ones = jnp.ones((16, 3 * RIM), jnp.bfloat16)
        mass = jnp.dot(ones, k_hi[t], preferred_element_type=jnp.float32)[0:1, :]
        for s in range(SETS):
            keep(1, s, t, scaled(0, s, t, mass))

    def arrive(k, s):
        for side in range(2):
            at = 0 if side == 0 else WIDE + cells

            @pl.when(has[side])
            def _():
                arrival(k, s, side).wait_recv()
                hi, lo = split(recv[k, s, side])
                values[0, s, 0:half, at : at + WIDE] = hi
                values[0, s, half:, at : at + WIDE] = lo

    def mass_of(parity, s, t):
        both = jnp.dot(
            values[parity, s, :, t * RIM : (t + 3) * RIM],
            k_hi[t],
            preferred_element_type=jnp.float32,
        )
        return both[0:half] + both[half:]

    def send_side(s, t):
        keep(1, s, t, scaled(0, s, t, mass_of(0, s, t)))

    def receive_side(k, s):
        for t in range(1, tiles + 1):
            w = scaled(1, s, t, mass_of(1, s, t))
            keep(0, s, t, w)
            if t <= 2:
                send[k, s, 0, :, (t - 1) * RIM : t * RIM] = w
            if t > tiles - 2:
                at = (t + 1 - tiles) * RIM
                send[k, s, 1, :, at : at + RIM] = w
        start(k, s)

    def finish(s, t):
        gathered = mass_of(1, s, t) + jnp.dot(
            values[1, s, 0:half, t * RIM : (t + 3) * RIM],
            k_lo[t],
            preferred_element_type=jnp.float32,
        )
        some = pl.ds(pl.multiple_of(s * half, half), half)
        flux_t[some, (t - 1) * RIM : t * RIM] = (
            scaled(1, s, t, gathered) * gathered
        )

    def turn(t):
        total = jnp.zeros((1, BLK), jnp.float32)
        for b in range(HB * t, HB * (t + 1)):
            out = flux_t[:, b * BLK : (b + 1) * BLK].T
            flux[b * BLK : (b + 1) * BLK, :] = out
            total = total + jnp.sum(out, axis=0, keepdims=True)
        return total

    pl.loop(0, SETS)(lambda s: receive_side(0, s))
    for k in range(ROUNDS):

        @pl.loop(0, SETS)
        def _(s):
            for t in range(2, tiles):
                send_side(s, t)

        @pl.loop(0, SETS)
        def _(s):
            arrive(k, s)
            for t in (0, 1, tiles, tiles + 1):
                send_side(s, t)
            if k + 1 < ROUNDS:
                receive_side(k + 1, s)
            else:
                for t in range(1, tiles + 1):
                    finish(s, t)

    totals = jnp.zeros((1, BLK), jnp.float32)
    for t in range(tiles):
        totals = totals + turn(t)

    sums[0, 0:1, :] = totals
    sums[0, 1:2, :] = live_count

    def sum_copy(d):
        return remote(
            sums.at[0],
            sums.at[d],
            sum_send_sem.at[d],
            sum_recv_sem.at[d],
            lax.rem(me + d, n),
        )

    @pl.loop(1, n)
    def _(d):
        sum_copy(d).start()

    out_copy = pltpu.make_async_copy(flux, flux_hbm, out_sem)
    out_copy.start()

    for side in range(2):

        @pl.when(has[side])
        def _():
            pos_copy(side).wait_send()
            lig_out(side).wait_send()
            for s in range(SETS):
                for k in range(ROUNDS):
                    copy_out(k, s, side).wait_send()

    @pl.loop(1, n)
    def _(d):
        sum_copy(d).wait()

    whole = jnp.sum(sums[...], axis=0)
    scale_ref[0:1, :] = whole[1:2, :] / whole[0:1, :]
    out_copy.wait()


def scale_kernel(flux_ref, scale_ref, out_ref):
    out_ref[...] = flux_ref[...] * scale_ref[...]


def body(positions, counts, ligands, receptors, lig_of_pair, rec_of_pair):
    n = lax.axis_size("tx")
    cells = positions.shape[1]
    nblock = counts.shape[0]
    tiles = cells // RIM
    pairs = lig_of_pair.shape[0]
    inside = cells + 2 * RIM
    wide = cells + 2 * WIDE
    half = pairs // SETS
    f32, bf16 = jnp.float32, jnp.bfloat16
    vmem = pl.BlockSpec(memory_space=pltpu.VMEM)
    smem = pl.BlockSpec(memory_space=pltpu.SMEM)
    hbm = pl.BlockSpec(memory_space=pltpu.HBM)
    flux, scale = pl.pallas_call(
        functools.partial(kernel, n),
        out_shape=(
            jax.ShapeDtypeStruct((cells, pairs), f32),
            jax.ShapeDtypeStruct((1, pairs), f32),
        ),
        in_specs=[hbm] * 6,
        out_specs=(hbm, vmem),
        scratch_shapes=[
            pltpu.VMEM(positions.shape, f32),
            pltpu.SMEM(counts.shape, jnp.int32),
            pltpu.VMEM((1, pairs), jnp.int32),
            pltpu.VMEM((1, pairs), jnp.int32),
            pltpu.VMEM((inside, ligands.shape[1]), f32),
            pltpu.VMEM(receptors.shape, f32),
            pltpu.VMEM((nblock + 2 * HB, 8, BLK), f32),
            pltpu.VMEM((nblock, 8, BLK), f32),
            pltpu.VMEM((2, REACH, 8, BLK), f32),
            pltpu.VMEM((2, REACH, 8, BLK), f32),
            pltpu.VMEM((wide, BLK), f32),
            pltpu.VMEM((wide, BLK), f32),
            pltpu.VMEM((1, inside), f32),
            pltpu.VMEM((tiles + 2, 3 * RIM, RIM), bf16),
            pltpu.VMEM((tiles + 2, 3 * RIM, RIM), bf16),
            pltpu.VMEM((2, pairs, inside), f32),
            pltpu.VMEM((2, SETS, 2 * half, wide), bf16),
            pltpu.VMEM((ROUNDS, SETS, 2, half, WIDE), f32),
            pltpu.VMEM((ROUNDS, SETS, 2, half, WIDE), f32),
            pltpu.VMEM((pairs, cells), f32),
            pltpu.VMEM((cells, pairs), f32),
            pltpu.VMEM((n, 2, BLK), f32),
            pltpu.SemaphoreType.DMA((6,)),
            pltpu.SemaphoreType.DMA,
            pltpu.SemaphoreType.DMA((2,)),
            pltpu.SemaphoreType.DMA((2,)),
            pltpu.SemaphoreType.DMA((2,)),
            pltpu.SemaphoreType.DMA((2,)),
            pltpu.SemaphoreType.DMA((ROUNDS, SETS, 2)),
            pltpu.SemaphoreType.DMA((ROUNDS, SETS, 2)),
            pltpu.SemaphoreType.DMA((n,)),
            pltpu.SemaphoreType.DMA((n,)),
        ],
        compiler_params=pltpu.CompilerParams(
            collective_id=0, has_side_effects=True
        ),
    )(
        positions,
        counts,
        lig_of_pair.reshape(1, pairs),
        rec_of_pair.reshape(1, pairs),
        ligands,
        receptors,
    )
    step = cells // 2
    return pl.pallas_call(
        scale_kernel,
        grid=(cells // step,),
        out_shape=jax.ShapeDtypeStruct((cells, pairs), f32),
        in_specs=[
            pl.BlockSpec((step, pairs), lambda i: (i, 0)),
            pl.BlockSpec((1, pairs), lambda i: (0, 0)),
        ],
        out_specs=pl.BlockSpec((step, pairs), lambda i: (i, 0)),
    )(flux, scale)


def solution(mesh):
    in_specs = (
        P(None, ("sections", "tx")),
        P(("sections", "tx")),
        P(("sections", "tx"), None),
        P(("sections", "tx"), None),
        P(),
        P(),
    )
    out_specs = P(("sections", "tx"), None)
    return jax.shard_map(body, mesh=mesh, in_specs=in_specs, out_specs=out_specs, check_vma=False)
```
